32 devices in a mesh: pos: 8 (over z, x), tile: 4 (over y, core).
Axes of the slice: x: 2, y: 2, z: 4, core: 2. Of those that a mesh axis runs over, the one named last changes fastest.
Arguments:
- object_field: float32 [2, 2048, 4096], P(None, 'tile', 'pos'), may hold values from -6 to 6
- probe: float32 [2, 256, 256], replicated, may hold values from -45 to 45
- amplitudes: bfloat16 [4, 8, 32, 256, 256], P('tile', 'pos'), may hold values from 0.099609375 to 3
- corner_rows: int32 [4, 8, 32], P('tile', 'pos'), may hold values from 0 to 511, as said below
- corner_cols: int32 [4, 8, 32], P('tile', 'pos'), may hold values from 0 to 511, as said below
- counts: int32 [4, 8], P('tile', 'pos'), may hold values from 1 to 32, as said below
Outputs:
- object_new: float32 [2, 2048, 4096], P(None, 'tile', 'pos')
- probe_grad: float32 [2, 256, 256], replicated
The draws below stay inside these ranges and needn't reach their ends.
Inputs may be any that keep to these rules, and one draw needn't show every extreme that they name: Slots from counts[t, p] on are unused. `corner_rows`: counted from the first row of the owner's block. `corner_cols`: counted from the first column of the owner's block.
All inputs are finite; a program needn't handle non-finite values.
Results may differ from the reference program's by a relative error of at most 0.0012.
Values sent between devices are 32-bit elements; how exact they have to be, the bound alone decides.
No kernel may reach another device: no remote copies, remote signals or barrier semaphores. Data moves between devices by JAX's collectives and lax.ppermute only.
A program may use at most 64 MiB of HBM per device.

```python
import math
import jax
import jax.numpy as jnp
from jax import lax

PATCH = 256
BLOCK_R = 512
BLOCK_C = 512
SLOTS = 32
TILES_T = 4
TILES_P = 8
ROWS_OBJ = 2048
COLS_OBJ = 4096


def draw_counts(key, part):
    first_key, second_key = jax.random.split(key)
    halvings = jax.random.randint(first_key, (TILES_T, TILES_P), 0, 4)
    levels = jnp.maximum(SLOTS // jnp.left_shift(jnp.ones((), jnp.int32), halvings), 1)
    chosen = jax.random.randint(second_key, (), 0, TILES_T * TILES_P)
    flat_levels = levels.reshape(TILES_T * TILES_P).at[chosen].set(SLOTS)
    return flat_levels.reshape(TILES_T, TILES_P).astype(jnp.int32)


def corner_draw(key, upper_end):
    first_key, second_key = jax.random.split(key)
    slot_total = TILES_T * TILES_P * SLOTS
    corners = jax.random.randint(first_key, (slot_total,), 0, upper_end)
    chosen = jax.random.randint(second_key, (), 0, slot_total)
    corners = corners.at[chosen].set(upper_end - 1).at[(chosen + 1) % slot_total].set(0)
    return corners.reshape(TILES_T, TILES_P, SLOTS).astype(jnp.int32)


def draw_corner_rows(key, part):
    return corner_draw(jax.random.fold_in(key, 11), BLOCK_R)


def draw_corner_cols(key, part):
    return corner_draw(jax.random.fold_in(key, 23), BLOCK_C)


def draw_probe(key, part):
    key_list = jax.random.split(jax.random.fold_in(key, 37), 3)
    log_low = math.log(0.3)
    log_high = math.log(3.0)
    row_scale = jnp.exp(jax.random.uniform(key_list[1], (1, PATCH, 1), jnp.float32, log_low, log_high))
    col_scale = jnp.exp(jax.random.uniform(key_list[2], (1, 1, PATCH), jnp.float32, log_low, log_high))
    entries = jnp.clip(jax.random.normal(key_list[0], (2, PATCH, PATCH), jnp.float32), -5.0, 5.0)
    return (entries * row_scale * col_scale).astype(jnp.float32)


def shard_levels(own_key, shape, cuts, least, top_value):
    loudness, own = 1.0, jax.random.fold_in(own_key, 6)
    for axis_at, blocks in cuts:
        heights = jnp.exp(jax.random.uniform(jax.random.fold_in(own, axis_at), (blocks,), jnp.float32, least / len(cuts), top_value / len(cuts)))
        loudness = loudness * jnp.repeat(heights, shape[axis_at] // blocks).reshape([-1 if axis == axis_at else 1 for axis in range(len(shape))])
    return loudness


def gaussian(stream_key, extent, scale, most, pieces=(), kind=jnp.bfloat16):
    values = jax.random.normal(stream_key, extent, jnp.float32) * scale
    if len(pieces) > 0:
        values = shard_levels(stream_key, extent, pieces, -0.22, 0.18) * values
    return jnp.clip(values, min=-most, max=most).astype(kind)


def setup_inputs(seed: int = 0) -> dict:
    splits = jax.random.split(jax.random.key(seed), 7)
    object_field = gaussian(splits[0], (2, ROWS_OBJ, COLS_OBJ), 1.0, 6.0, ((1, 4), (2, 8)), jnp.float32)
    probe = draw_probe(jax.random.fold_in(splits[6], 71), 0)
    amplitudes = jnp.clip(jnp.exp(math.log(3.0) - 3.4051113 * jax.random.uniform(splits[2], (TILES_T, TILES_P, SLOTS, PATCH, PATCH), jnp.float32) ** shard_levels(splits[2], (TILES_T, TILES_P, SLOTS, PATCH, PATCH), ((0, 4), (1, 8)), -0.2, 0.2)), 0.099609375, 3.0).astype(jnp.bfloat16)
    corner_rows = draw_corner_rows(jax.random.fold_in(splits[6], 71), 0)
    corner_cols = draw_corner_cols(jax.random.fold_in(splits[6], 71), 0)
    counts = draw_counts(jax.random.fold_in(splits[6], 71), 0)
    return {"object_field": object_field, "probe": probe, "amplitudes": amplitudes, "corner_rows": corner_rows, "corner_cols": corner_cols, "counts": counts}


def dft_tables(points):
    indices = jnp.arange(points, dtype=jnp.int32)
    residues = indices[:, None] * indices[None, :] % points
    angles = residues.astype(jnp.float32) * (2.0 * math.pi / points)
    factor = 1.0 / math.sqrt(points)
    return ((jnp.cos(angles) * factor).astype(jnp.bfloat16), (-jnp.sin(angles) * factor).astype(jnp.bfloat16))

def left_product(table_re, table_im, part_re, part_im):

    def product(matrix, operand):
        return jnp.dot(matrix, operand, preferred_element_type=jnp.float32)
    return (product(table_re, part_re) - product(table_im, part_im), product(table_re, part_im) + product(table_im, part_re))

def right_product(part_re, part_im, table_re, table_im):

    def product(operand, matrix):
        return jnp.dot(operand, matrix, preferred_element_type=jnp.float32)
    return (product(part_re, table_re) - product(part_im, table_im), product(part_re, table_im) + product(part_im, table_re))

def propagate(exit_re, exit_im, amplitude, table_re, table_im):
    near_re, near_im = left_product(table_re, table_im, exit_re.astype(jnp.bfloat16), exit_im.astype(jnp.bfloat16))
    far_re, far_im = right_product(near_re.astype(jnp.bfloat16), near_im.astype(jnp.bfloat16), table_re, table_im)
    modulus = jnp.sqrt(far_re * far_re + far_im * far_im + 0.25)
    ratio = amplitude.astype(jnp.float32) / modulus
    back_re, back_im = left_product(table_re, -table_im, (far_re * ratio).astype(jnp.bfloat16), (far_im * ratio).astype(jnp.bfloat16))
    new_re, new_im = right_product(back_re.astype(jnp.bfloat16), back_im.astype(jnp.bfloat16), table_re, -table_im)
    return (new_re - exit_re, new_im - exit_im)

def reference(object_field, probe, amplitudes, corner_rows, corner_cols, counts):
    table_re, table_im = dft_tables(PATCH)
    padded = jnp.pad(object_field, ((0, 0), (0, PATCH), (0, PATCH)))
    per_owner = TILES_P * SLOTS
    total_slots = TILES_T * per_owner
    probe_re, probe_im = (probe[0], probe[1])

    def slot_terms(operands):
        patch_re, patch_im, amplitude = operands
        exit_re = probe_re * patch_re - probe_im * patch_im
        exit_im = probe_re * patch_im + probe_im * patch_re
        delta_re, delta_im = propagate(exit_re, exit_im, amplitude, table_re, table_im)
        object_part = jnp.stack([probe_re * delta_re + probe_im * delta_im, probe_re * delta_im - probe_im * delta_re])
        probe_part = jnp.stack([patch_re * delta_re + patch_im * delta_im, patch_re * delta_im - patch_im * delta_re])
        return (object_part, probe_part)

    def skip_terms(operands):
        zeros_pair = jnp.zeros((2, PATCH, PATCH), jnp.float32)
        return (zeros_pair, zeros_pair)

    def visit(slot_index, state_pair):
        update, probe_sum = state_pair
        slot_index = slot_index.astype(jnp.int32)
        owner_t = slot_index // per_owner
        owner_p = slot_index // SLOTS % TILES_P
        slot_pos = slot_index % SLOTS
        row_start = (owner_t * BLOCK_R + corner_rows[owner_t, owner_p, slot_pos]).astype(jnp.int32)
        col_start = (owner_p * BLOCK_C + corner_cols[owner_t, owner_p, slot_pos]).astype(jnp.int32)
        zero_index = jnp.zeros((), jnp.int32)
        window = lax.dynamic_slice(padded, (zero_index, row_start, col_start), (2, PATCH, PATCH))
        amplitude = amplitudes[owner_t, owner_p, slot_pos]
        object_part, probe_part = lax.cond(slot_pos < counts[owner_t, owner_p], slot_terms, skip_terms, (window[0], window[1], amplitude))
        current = lax.dynamic_slice(update, (zero_index, row_start, col_start), (2, PATCH, PATCH))
        update = lax.dynamic_update_slice(update, current + object_part, (zero_index, row_start, col_start))
        return (update, probe_sum + probe_part)
    start_state = (jnp.zeros(padded.shape, jnp.float32), jnp.zeros((2, PATCH, PATCH), jnp.float32))
    update, probe_sum = lax.fori_loop(0, total_slots, visit, start_state)
    update = update[:, :ROWS_OBJ, :COLS_OBJ]
    power = jnp.mean(probe_re * probe_re + probe_im * probe_im) + 1e-06
    object_new = object_field + update / power
    probe_grad = probe_sum / math.sqrt(total_slots)
    return (object_new, probe_grad)
```

```python
import functools
import math

import jax
import jax.numpy as jnp
import numpy as np
from jax import lax
from jax.experimental import pallas as pl
from jax.experimental.pallas import tpu as pltpu
from jax.sharding import PartitionSpec as P

LANES = 128
ROWS_STEP = 32


def passed_along(block, axis, distance):
    devices = range(lax.axis_size(axis))
    route = [(i - distance, i) for i in devices if i - distance in devices]
    return lax.ppermute(block, axis, route)


def dft_blocks(points):
    indices = np.arange(points)
    angles = (indices[:, None] * indices[None, :] % points) * (2.0 * math.pi / points)
    factor = 1.0 / math.sqrt(points)
    real = (np.cos(angles) * factor).astype(jnp.bfloat16)
    imag = (-np.sin(angles) * factor).astype(jnp.bfloat16)
    left = np.block([[real, -imag], [imag, real]])
    right = np.block([[real, imag], [-imag, real]])
    return jnp.asarray(left), jnp.asarray(right)


def dot(a, b):
    return jnp.dot(a, b, preferred_element_type=jnp.float32)


def collect(keep, slot_total, order_ref):
    def look(slot, found):
        order_ref[found] = slot
        return found + keep(slot).astype(jnp.int32)

    found = lax.fori_loop(0, slot_total, look, jnp.int32(0))

    order_ref[found] = order_ref[jnp.maximum(found - 1, 0)]
    return found


def run_slots(found, order_ref, rows_ref, cols_ref, probe_ref, amp_ref, left_ref, right_ref,
              field, update, probe_sum, patch, exits, stack, wide):
    size = probe_ref.shape[1]
    blocks = size // LANES

    def read(which, slot):
        row = rows_ref[slot]
        col = cols_ref[slot]
        base = col // LANES
        shift = col % LANES
        for at in range(0, size, ROWS_STEP):
            rows = pl.ds(at, ROWS_STEP)
            lanes = lax.broadcasted_iota(jnp.int32, (ROWS_STEP, LANES), 1)
            own = lanes < LANES - shift
            for block in range(blocks):
                cols = pl.ds(block * LANES, LANES)
                part = []
                for plane in range(2):
                    pair = [
                        pltpu.roll(
                            field[plane, base + k, pl.ds(row + at, ROWS_STEP), :],
                            LANES - shift, 1)
                        for k in (block, block + 1)
                    ]
                    part.append(jnp.where(own, pair[0], pair[1]))
                    patch[which, plane, rows, cols] = part[plane]
                probe_re = probe_ref[0, rows, cols]
                probe_im = probe_ref[1, rows, cols]
                exit_re = probe_re * part[0] - probe_im * part[1]
                exit_im = probe_re * part[1] + probe_im * part[0]
                exits[which, 0, rows, cols] = exit_re
                exits[which, 1, rows, cols] = exit_im
                spot = pl.ds(which * size + block * LANES, LANES)
                stack[rows, spot] = exit_re.astype(jnp.bfloat16)
                stack[pl.ds(size + at, ROWS_STEP), spot] = exit_im.astype(jnp.bfloat16)

    def turn(product):
        for which in range(2):
            for plane in range(2):
                wide[pl.ds(which * size, size), pl.ds(plane * size, size)] = product[
                    plane * size:(plane + 1) * size, which * size:(which + 1) * size
                ].astype(jnp.bfloat16)

    def fix(far, which, slot):
        far_re = far[which * size:(which + 1) * size, :size]
        far_im = far[which * size:(which + 1) * size, size:]
        amp = amp_ref[slot].astype(jnp.float32)
        ratio = amp * lax.rsqrt(far_re * far_re + far_im * far_im + 0.25)
        spot = pl.ds(which * size, size)
        stack[pl.ds(0, size), spot] = (far_re * ratio).astype(jnp.bfloat16)
        stack[pl.ds(size, size), spot] = (far_im * ratio).astype(jnp.bfloat16)

    def add(new, which, slot, weight):
        row = rows_ref[slot]
        col = cols_ref[slot]
        base = col // LANES
        shift = col % LANES
        for at in range(0, size, ROWS_STEP):
            rows = pl.ds(at, ROWS_STEP)
            lanes = lax.broadcasted_iota(jnp.int32, (ROWS_STEP, LANES), 1)
            own = lanes >= shift
            terms = [[], []]
            for block in range(blocks):
                cols = pl.ds(block * LANES, LANES)
                delta = []
                for plane in range(2):
                    start = plane * size + block * LANES
                    value = new[which * size + at:which * size + at + ROWS_STEP, start:start + LANES]
                    value = value - exits[which, plane, rows, cols]
                    delta.append(value if weight is None else value * weight)
                probe_re = probe_ref[0, rows, cols]
                probe_im = probe_ref[1, rows, cols]
                patch_re = patch[which, 0, rows, cols]
                patch_im = patch[which, 1, rows, cols]
                terms[0].append(pltpu.roll(probe_re * delta[0] + probe_im * delta[1], shift, 1))
                terms[1].append(pltpu.roll(probe_re * delta[1] - probe_im * delta[0], shift, 1))
                probe_sum[0, rows, cols] += patch_re * delta[0] + patch_im * delta[1]
                probe_sum[1, rows, cols] += patch_re * delta[1] - patch_im * delta[0]
            for plane in range(2):
                rolled = terms[plane]
                for k in range(blocks + 1):
                    if k == 0:
                        value = jnp.where(own, rolled[0], 0.0)
                    elif k == blocks:
                        value = jnp.where(own, 0.0, rolled[blocks - 1])
                    else:
                        value = jnp.where(own, rolled[k], rolled[k - 1])
                    update[plane, base + k, pl.ds(row + at, ROWS_STEP), :] += value

    def pair_step(step, carry):
        first = order_ref[2 * step]
        second = order_ref[2 * step + 1]
        weight = jnp.where(2 * step + 1 < found, 1.0, 0.0).astype(jnp.float32)
        read(0, first)
        read(1, second)
        turn(dot(left_ref[...], stack[...]))
        far = dot(wide[...], right_ref[...])
        fix(far, 0, first)
        fix(far, 1, second)
        turn(dot(right_ref[...], stack[...]))
        new = dot(wide[...], left_ref[...])
        add(new, 0, first, None)
        add(new, 1, second, weight)
        return carry

    lax.fori_loop(0, (found + 1) // 2, pair_step, 0)


def put(into, row, col, value):
    rows, cols = value.shape[1:]
    for block in range(cols // LANES):
        into[:, col // LANES + block, row:row + rows, :] = value[:, :, block * LANES:(block + 1) * LANES]


def take(out, source, row, col):
    rows, cols = out.shape[1:]
    for block in range(cols // LANES):
        out[:, :, block * LANES:(block + 1) * LANES] = source[:, col // LANES + block, row:row + rows, :]


def near_kernel(rows_ref, cols_ref, count_ref, block_ref, lower_ref, probe_ref, amp_ref, left_ref, right_ref,
                update, probe_sum, order_ref, field, patch, exits, stack, wide):
    size = probe_ref.shape[1]
    rows_here, cols_here = block_ref.shape[1:]
    put(field, 0, 0, block_ref)
    put(field, rows_here, 0, lower_ref)
    update[...] = jnp.zeros_like(update)
    probe_sum[...] = jnp.zeros_like(probe_sum)
    live = count_ref[0]
    found = collect(lambda slot: (slot < live) & (cols_ref[slot] < cols_here - size), rows_ref.shape[0], order_ref)
    run_slots(found, order_ref, rows_ref, cols_ref, probe_ref, amp_ref, left_ref, right_ref,
              field, update, probe_sum, patch, exits, stack, wide)


def rim_kernel(rows_ref, cols_ref, count_ref, block_ref, lower_ref, right_top_ref, right_low_ref, corner_ref,
               probe_ref, amp_ref, left_ref, right_ref, update_in, probe_in,
               own_out, lower_out, right_top_out, right_low_out, corner_out, probe_sum,
               order_ref, field, update, patch, exits, stack, wide):
    size = probe_ref.shape[1]
    rows_here, cols_here = block_ref.shape[1:]
    put(field, 0, 0, block_ref)
    put(field, rows_here, 0, lower_ref)
    put(field, 0, cols_here, right_top_ref)
    put(field, size, cols_here, right_low_ref)
    put(field, rows_here, cols_here, corner_ref)
    inner = cols_here // LANES
    update[:, :inner] = update_in[...]
    update[:, inner:] = jnp.zeros((2, size // LANES) + update.shape[2:], jnp.float32)
    probe_sum[...] = probe_in[...]
    live = count_ref[0]
    found = collect(lambda slot: (slot < live) & (cols_ref[slot] >= cols_here - size), rows_ref.shape[0], order_ref)
    run_slots(found, order_ref, rows_ref, cols_ref, probe_ref, amp_ref, left_ref, right_ref,
              field, update, probe_sum, patch, exits, stack, wide)
    take(own_out, update, 0, 0)
    take(lower_out, update, rows_here, 0)
    take(right_top_out, update, 0, cols_here)
    take(right_low_out, update, size, cols_here)
    take(corner_out, update, rows_here, cols_here)


def finish_kernel(block_ref, own_ref, lower_ref, right_top_ref, right_low_ref, probe_ref, out_ref):
    size = probe_ref.shape[1]
    probe_re = probe_ref[0]
    probe_im = probe_ref[1]
    power = jnp.mean(probe_re * probe_re + probe_im * probe_im) + 1e-06
    scale = 1.0 / power
    for plane in range(2):
        top = own_ref[plane, :size, :] + lower_ref[plane]
        low = own_ref[plane, size:, :]
        out_ref[plane, :size, size:] = block_ref[plane, :size, size:] + top[:, size:] * scale
        out_ref[plane, :size, :size] = block_ref[plane, :size, :size] + (top[:, :size] + right_top_ref[plane]) * scale
        out_ref[plane, size:, size:] = block_ref[plane, size:, size:] + low[:, size:] * scale
        out_ref[plane, size:, :size] = block_ref[plane, size:, :size] + (low[:, :size] + right_low_ref[plane]) * scale


def summed_everywhere(value):
    steps = []
    for axis in ("tile", "pos"):
        size = lax.axis_size(axis)
        masks = []
        mask = 1
        while mask < size:
            masks.append((axis, mask))
            mask *= 2
        steps += masks if axis == "tile" else masks[::-1]

    def partner(block, axis, mask):
        return lax.ppermute(block, axis, [(i, i ^ mask) for i in range(lax.axis_size(axis))])

    def is_low(axis, mask):
        return lax.axis_index(axis) // mask % 2 == 0

    halved = steps[:-2]
    for axis, mask in halved:
        half = value.shape[0] // 2
        low = is_low(axis, mask)
        kept = jnp.where(low, value[:half], value[half:])
        given = jnp.where(low, value[half:], value[:half])
        value = kept + partner(given, axis, mask)
    for axis, mask in steps[-2:]:
        value = value + partner(value, axis, mask)
    for axis, mask in halved[::-1]:
        other = partner(value, axis, mask)
        low = is_low(axis, mask)
        value = jnp.where(low, jnp.concatenate([value, other]), jnp.concatenate([other, value]))
    return value


def shards(object_field, probe, amplitudes, corner_rows, corner_cols, counts):
    size = probe.shape[1]
    rows_here = object_field.shape[1]
    cols_here = object_field.shape[2]
    slots = corner_rows.shape[2]
    left, right = dft_blocks(size)
    slot_rows = corner_rows.reshape(slots)
    slot_cols = corner_cols.reshape(slots)
    live_count = counts.reshape(1)
    amps = amplitudes.reshape(slots, size, size)

    right_top = passed_along(object_field[:, :size, :size], "pos", -1)
    lower = passed_along(object_field[:, :size, :], "tile", -1)
    right_low = passed_along(object_field[:, size:, :size], "pos", -1)
    corner = passed_along(right_top, "tile", -1)

    def spec(n, smem):
        return [pl.BlockSpec(memory_space=pltpu.SMEM)] * smem + [pl.BlockSpec(memory_space=pltpu.VMEM)] * (n - smem)

    def f32(*shape):
        return jax.ShapeDtypeStruct(shape, jnp.float32)

    def work(cols):
        return [
            pltpu.SMEM((slots + 1,), jnp.int32),
            pltpu.VMEM((2, cols // LANES, rows_here + size, LANES), jnp.float32),
        ], [
            pltpu.VMEM((2, 2, size, size), jnp.float32),
            pltpu.VMEM((2, 2, size, size), jnp.float32),
            pltpu.VMEM((2 * size, 2 * size), jnp.bfloat16),
            pltpu.VMEM((2 * size, 2 * size), jnp.bfloat16),
        ]

    def cost(parts):
        return pl.CostEstimate(
            flops=slots // parts * 32 * size**3, bytes_accessed=8 * size * size * slots, transcendentals=0)

    params = pltpu.CompilerParams(vmem_limit_bytes=40 * 1024 * 1024)
    before, after = work(cols_here)
    update, probe_sum = pl.pallas_call(
        near_kernel,
        out_shape=(f32(2, cols_here // LANES, rows_here + size, LANES), f32(2, size, size)),
        in_specs=spec(9, 3),
        out_specs=(pl.BlockSpec(memory_space=pltpu.VMEM),) * 2,
        scratch_shapes=before + after,
        compiler_params=params,
        cost_estimate=cost(2),
        name="near_slots",
    )(slot_rows, slot_cols, live_count, object_field, lower, probe, amps, left, right)

    before, after = work(cols_here + size)
    own, low_part, top_part, side_part, corner_part, probe_sum = pl.pallas_call(
        rim_kernel,
        out_shape=(
            f32(2, rows_here, cols_here), f32(2, size, cols_here), f32(2, size, size),
            f32(2, rows_here - size, size), f32(2, size, size), f32(2, size, size)),
        in_specs=spec(14, 3),
        out_specs=(pl.BlockSpec(memory_space=pltpu.VMEM),) * 6,
        scratch_shapes=before + before[1:] + after,
        compiler_params=params,
        cost_estimate=cost(2),
        name="rim_slots",
    )(slot_rows, slot_cols, live_count, object_field, lower, right_top, right_low, corner,
      probe, amps, left, right, update, probe_sum)

    corner_back = passed_along(corner_part, "tile", 1)
    side_back = passed_along(side_part, "pos", 1)
    low_back = passed_along(low_part, "tile", 1)
    top_back = passed_along(top_part + corner_back, "pos", 1)

    total = summed_everywhere(probe_sum.reshape(2 * size, size)).reshape(2, size, size)
    probe_grad = total / math.sqrt(lax.axis_size("pos") * lax.axis_size("tile") * slots)

    object_new = pl.pallas_call(
        finish_kernel,
        out_shape=f32(2, rows_here, cols_here),
        in_specs=spec(6, 0),
        out_specs=pl.BlockSpec(memory_space=pltpu.VMEM),
        compiler_params=params,
        name="finish",
    )(object_field, own, low_back, top_back, side_back, probe)
    return (object_new, probe_grad)


def solution(mesh):
    return jax.shard_map(
        shards,
        mesh=mesh,
        in_specs=(
            P(None, "tile", "pos"),
            P(),
            P("tile", "pos", None, None, None),
            P("tile", "pos", None),
            P("tile", "pos", None),
            P("tile", "pos"),
        ),
        out_specs=(P(None, "tile", "pos"), P()),
        check_vma=False,
    )
```

```python
import math

import jax
import jax.numpy as jnp
import numpy as np
from jax import lax
from jax.experimental import pallas as pl
from jax.experimental.pallas import tpu as pltpu
from jax.sharding import PartitionSpec as P

LANES = 128
STEP = 32
GROUP = 2


def passed_along(block, axis, distance):
    devices = range(lax.axis_size(axis))
    route = [(i - distance, i) for i in devices if i - distance in devices]
    return lax.ppermute(block, axis, route)


def dft_blocks(points):
    indices = np.arange(points)
    angles = (indices[:, None] * indices[None, :] % points) * (2.0 * math.pi / points)
    factor = 1.0 / math.sqrt(points)
    table_re, table_im = np.cos(angles) * factor, -np.sin(angles) * factor

    def left(rows, cols, sign):
        re, im = table_re[rows, cols], sign * table_im[rows, cols]
        return np.block([[re, -im], [im, re]])

    def right(rows, cols, sign):
        re, im = table_re[rows, cols], sign * table_im[rows, cols]
        return np.block([[re, im], [-im, re]])

    low, even, odd = slice(0, points // 2), slice(0, None, 2), slice(1, None, 2)
    order = np.concatenate([indices[even], indices[odd]])
    sort = np.zeros((points, points))
    sort[indices, order] = 1.0
    return np.stack([
        left(even, low, 1), left(odd, low, 1), right(low, even, 1), right(low, odd, 1),
        left(low, even, -1), left(low, odd, -1), right(even, low, -1), right(odd, low, -1),
        sort, sort.T,
    ]).astype(jnp.bfloat16)


def dot(a, b):
    return jnp.dot(a, b, preferred_element_type=jnp.float32)


def collect(keep, slot_total, order_ref):
    def look(slot, found):
        order_ref[found] = slot
        return found + keep(slot).astype(jnp.int32)

    found = lax.fori_loop(0, slot_total, look, jnp.int32(0))
    last = order_ref[jnp.maximum(found - 1, 0)]
    for extra in range(GROUP - 1):
        order_ref[found + extra] = last
    return found


def run_slots(found, order_ref, rows_ref, cols_ref, probe_ref, amp_ref, mats,
              field, update, probe_sum, scratch):
    size = probe_ref.shape[1]
    half = size // 2
    bf16 = jnp.bfloat16
    patch, xs, far, gs = scratch

    def place(slot):
        col = cols_ref[slot]
        return rows_ref[slot], col // LANES, col % LANES

    def times(re, im, other_re, other_im):
        return re * other_re - im * other_im, re * other_im + im * other_re

    def read(which, slot):
        row, base, shift = place(slot)
        own = lax.broadcasted_iota(jnp.int32, (STEP, LANES), 1) < LANES - shift
        for at in range(0, half, STEP):
            rounded = [[None, None], [None, None]]
            for low in range(2):
                top = low * half + at
                rows = slice(top, top + STEP)
                part = [[None, None], [None, None]]
                for plane in range(2):
                    rolled = [pltpu.roll(field[plane, base + k, pl.ds(row + top, STEP), :], LANES - shift, 1) for k in range(3)]
                    for block in range(2):
                        part[block][plane] = jnp.where(own, rolled[block], rolled[block + 1])
                        patch[which, plane, rows, block * LANES:(block + 1) * LANES] = part[block][plane]
                for block in range(2):
                    cols = slice(block * LANES, (block + 1) * LANES)
                    re, im = times(probe_ref[0, rows, cols], probe_ref[1, rows, cols], *part[block])
                    rounded[block][low] = (re.astype(bf16), im.astype(bf16))
            for block in range(2):
                cols = slice(which * size + block * LANES, which * size + (block + 1) * LANES)
                for plane in range(2):
                    up, low = rounded[block][0][plane], rounded[block][1][plane]
                    rows = slice(plane * half + at, plane * half + at + STEP)
                    xs[0, rows, cols] = up + low
                    xs[1, rows, cols] = up - low

    def group_step(step, carry):
        slots = [order_ref[GROUP * step + i] for i in range(GROUP)]
        for which in range(GROUP):
            read(which, slots[which])
        near = [dot(mats[parity], xs[parity]).astype(bf16) for parity in range(2)]
        folds = [[], []]
        for which in range(GROUP):
            for parity in range(2):
                left = near[parity][:, which * size:which * size + half]
                right = near[parity][:, which * size + half:(which + 1) * size]
                for sign, both in enumerate((left + right, left - right)):
                    folds[sign].append(jnp.concatenate([both[:half], both[half:]], axis=1))
        for sign in range(2):
            far[sign] = dot(jnp.concatenate(folds[sign], axis=0), mats[2 + sign])
        for which in range(GROUP):
            for at in range(0, size, STEP):
                rows = slice(which * size + at, which * size + at + STEP)
                for block in range(2):
                    re = far[block, rows, :half]
                    im = far[block, rows, half:]
                    amp = amp_ref[slots[which], at:at + STEP, block * LANES:(block + 1) * LANES].astype(jnp.float32)
                    ratio = amp * lax.rsqrt(re * re + im * im + 0.25)
                    down = at % half
                    cols = slice(which * size + block * LANES, which * size + (block + 1) * LANES)
                    gs[at // half, down:down + STEP, cols] = (re * ratio).astype(bf16)
                    gs[at // half, half + down:half + down + STEP, cols] = (im * ratio).astype(bf16)
        even = dot(mats[4], gs[0])
        odd = dot(mats[5], gs[1])
        back = (even + odd).astype(bf16), (even - odd).astype(bf16)
        sums = []
        for parity in range(2):
            parts = []
            for which in range(GROUP):
                cols = slice(which * size + parity * half, which * size + (parity + 1) * half)
                for value in back:
                    parts.append(jnp.concatenate([value[:half, cols], value[half:, cols]], axis=1))
            sums.append(dot(jnp.concatenate(parts, axis=0), mats[6 + parity]))
        places = [place(slot) for slot in slots]
        weights = [None] + [jnp.where(GROUP * step + i < found, 1.0, 0.0).astype(jnp.float32) for i in range(1, GROUP)]
        for at in range(0, size, STEP):
            rows = slice(at, at + STEP)
            terms = [[[], []] for _ in range(GROUP)]
            for block in range(2):
                cols = slice(block * LANES, (block + 1) * LANES)
                probe_re = probe_ref[0, rows, cols]
                probe_im = probe_ref[1, rows, cols]
                total = None
                for which in range(GROUP):
                    patch_re = patch[which, 0, rows, cols]
                    patch_im = patch[which, 1, rows, cols]
                    delta = []
                    for plane, value in enumerate(times(probe_re, probe_im, patch_re, patch_im)):
                        a = sums[0][which * size + at:which * size + at + STEP, plane * half:(plane + 1) * half]
                        b = sums[1][which * size + at:which * size + at + STEP, plane * half:(plane + 1) * half]
                        value = (a + b if block == 0 else a - b) - value
                        delta.append(value if which == 0 else value * weights[which])
                    shift = places[which][2]
                    terms[which][0].append(pltpu.roll(probe_re * delta[0] + probe_im * delta[1], shift, 1))
                    terms[which][1].append(pltpu.roll(probe_re * delta[1] - probe_im * delta[0], shift, 1))
                    own_sum = patch_re * delta[0] + patch_im * delta[1], patch_re * delta[1] - patch_im * delta[0]
                    total = own_sum if total is None else (total[0] + own_sum[0], total[1] + own_sum[1])
                probe_sum[0, rows, cols] += total[0]
                probe_sum[1, rows, cols] += total[1]
            for which in range(GROUP):
                row, base, shift = places[which]
                own = lax.broadcasted_iota(jnp.int32, (STEP, LANES), 1) >= shift
                for plane in range(2):
                    first, second = terms[which][plane]
                    update[plane, base, pl.ds(row + at, STEP), :] += jnp.where(own, first, 0.0)
                    update[plane, base + 1, pl.ds(row + at, STEP), :] += jnp.where(own, second, first)
                    update[plane, base + 2, pl.ds(row + at, STEP), :] += jnp.where(own, 0.0, second)
        return carry

    lax.fori_loop(0, (found + GROUP - 1) // GROUP, group_step, 0)


def put(into, row, col, value):
    rows, cols = value.shape[1:]
    for block in range(cols // LANES):
        into[:, col // LANES + block, row:row + rows, :] = value[:, :, block * LANES:(block + 1) * LANES]


def inner_kernel(rows_ref, cols_ref, count_ref, block_ref, probe_ref, amps_ref, mats,
                 update, probe_sum, amp_ref, order_ref, field, *scratch):
    size = probe_ref.shape[1]
    rows_here, cols_here = block_ref.shape[1:]
    put(field, 0, 0, block_ref)
    update[...] = jnp.zeros_like(update)
    probe_sum[...] = jnp.zeros_like(probe_sum)
    live = count_ref[0]
    total = rows_ref.shape[0]
    batch = math.gcd(4, total)

    def sort_amps(step, carry):
        taken = [amps_ref[step * batch + i] for i in range(batch)]
        taken = [dot(mats[8], value).astype(jnp.bfloat16) for value in taken]
        for i in range(batch):
            amp_ref[step * batch + i] = dot(taken[i], mats[9]).astype(jnp.bfloat16)
        return carry

    lax.fori_loop(0, (live + batch - 1) // batch, sort_amps, 0)

    def keep(slot):
        return (slot < live) & (cols_ref[slot] < cols_here - size) & (rows_ref[slot] <= rows_here - size)

    found = collect(keep, total, order_ref)
    run_slots(found, order_ref, rows_ref, cols_ref, probe_ref, amp_ref, mats, field, update, probe_sum, scratch)


def right_kernel(rows_ref, cols_ref, count_ref, block_ref, lower_ref, top_ref, side_ref, corner_ref,
                 probe_ref, amp_ref, mats, update_in, probe_in,
                 update_out, probe_sum, top_out, side_out, corner_out, order_ref, field, update, *scratch):
    size = probe_ref.shape[1]
    rows_here, cols_here = block_ref.shape[1:]
    edge = cols_here // LANES
    put(field, 0, 0, block_ref)
    put(field, rows_here, 0, lower_ref)
    put(field, 0, cols_here, top_ref)
    put(field, size, cols_here, side_ref)
    put(field, rows_here, cols_here, corner_ref)
    update[:, :edge, :rows_here, :] = update_in[...]
    update[:, :edge, rows_here:, :] = jnp.zeros((2, edge, size, LANES), jnp.float32)
    update[:, edge:, :, :] = jnp.zeros((2, size // LANES, rows_here + size, LANES), jnp.float32)
    probe_sum[...] = probe_in[...]
    live = count_ref[0]
    found = collect(lambda slot: (slot < live) & (cols_ref[slot] >= cols_here - size), rows_ref.shape[0], order_ref)
    run_slots(found, order_ref, rows_ref, cols_ref, probe_ref, amp_ref, mats, field, update, probe_sum, scratch)
    update_out[...] = update[:, :edge, :, :]
    top_out[...] = update[:, edge:, :size, :]
    side_out[...] = update[:, edge:, size:rows_here, :]
    corner_out[...] = update[:, edge:, rows_here:, :]


def lower_kernel(rows_ref, cols_ref, count_ref, block_ref, lower_ref, probe_ref, amp_ref, mats, update_in, probe_in,
                 update, low_out, probe_sum, order_ref, field, *scratch):
    size = probe_ref.shape[1]
    rows_here, cols_here = block_ref.shape[1:]
    put(field, 0, 0, block_ref)
    put(field, rows_here, 0, lower_ref)
    update[...] = update_in[...]
    probe_sum[...] = probe_in[...]
    live = count_ref[0]

    def keep(slot):
        return (slot < live) & (cols_ref[slot] < cols_here - size) & (rows_ref[slot] > rows_here - size)

    found = collect(keep, rows_ref.shape[0], order_ref)
    run_slots(found, order_ref, rows_ref, cols_ref, probe_ref, amp_ref, mats, field, update, probe_sum, scratch)
    low_out[...] = update[:, :, rows_here:, :]


def tie_kernel(value_in, other_in, value_out):
    pass


def tie(value, other):
    anywhere = pl.BlockSpec(memory_space=pl.ANY)
    return pl.pallas_call(
        tie_kernel,
        out_shape=jax.ShapeDtypeStruct(value.shape, value.dtype),
        in_specs=[anywhere] * 2,
        out_specs=anywhere,
        input_output_aliases={0: 0},
        compiler_params=pltpu.CompilerParams(vmem_limit_bytes=1024 * 1024),
        name="tie",
    )(value, other)


def finish_kernel(block_ref, update, low_ref, top_ref, side_ref, probe_ref, out_ref):
    size = probe_ref.shape[1]
    rows_here, cols_here = block_ref.shape[1:]
    probe_re = probe_ref[0]
    probe_im = probe_ref[1]
    scale = 1.0 / (jnp.mean(probe_re * probe_re + probe_im * probe_im) + 1e-06)
    for plane in range(2):
        for block in range(cols_here // LANES):
            cols = slice(block * LANES, (block + 1) * LANES)
            top = update[plane, block, :size, :] + low_ref[plane, block]
            side = update[plane, block, size:rows_here, :]
            if block < size // LANES:
                top = top + top_ref[plane, block]
                side = side + side_ref[plane, block]
            out_ref[plane, :size, cols] = block_ref[plane, :size, cols] + top * scale
            out_ref[plane, size:, cols] = block_ref[plane, size:, cols] + side * scale


def partner(block, axis, mask):
    return lax.ppermute(block, axis, [(i, i ^ mask) for i in range(lax.axis_size(axis))])


def is_low(axis, mask):
    return lax.axis_index(axis) // mask % 2 == 0


def halve(value, axis, mask):
    half = value.shape[0] // 2
    low = is_low(axis, mask)
    kept = jnp.where(low, value[:half], value[half:])
    given = jnp.where(low, value[half:], value[:half])
    return kept + partner(given, axis, mask)


def rejoin(value, axis, mask):
    other = partner(value, axis, mask)
    return jnp.where(is_low(axis, mask), jnp.concatenate([value, other]), jnp.concatenate([other, value]))


def masks_of(axis):
    masks = []
    while 2 ** len(masks) < lax.axis_size(axis):
        masks.append((axis, 2 ** len(masks)))
    return masks


def shards(object_field, probe, amplitudes, corner_rows, corner_cols, counts):
    size = probe.shape[1]
    rows_here = object_field.shape[1]
    cols_here = object_field.shape[2]
    slots = corner_rows.shape[2]
    mats = jnp.asarray(dft_blocks(size))
    slot_rows = corner_rows.reshape(slots)
    slot_cols = corner_cols.reshape(slots)
    live_count = counts.reshape(1)
    amps = amplitudes.reshape(slots, size, size)

    right_top = passed_along(object_field[:, :size, :size], "pos", -1)
    right_side = passed_along(object_field[:, size:, :size], "pos", -1)
    lower = passed_along(object_field[:, :size, :], "tile", -1)
    smem = pl.BlockSpec(memory_space=pltpu.SMEM)
    vmem = pl.BlockSpec(memory_space=pltpu.VMEM)

    def f32(*shape):
        return jax.ShapeDtypeStruct(shape, jnp.float32)

    def scratch(blocks, rows, kept):
        held = pltpu.VMEM((2, blocks, rows, LANES), jnp.float32)
        return [pltpu.SMEM((slots + GROUP,), jnp.int32)] + [held] * kept + [
            pltpu.VMEM((GROUP, 2, size, size), jnp.float32),
            pltpu.VMEM((2, size, GROUP * size), jnp.bfloat16),
            pltpu.VMEM((2, GROUP * size, size), jnp.float32),
            pltpu.VMEM((2, size, GROUP * size), jnp.bfloat16),
        ]

    def call(kernel, name, outs, held, *arrays):
        return pl.pallas_call(
            kernel,
            out_shape=outs,
            in_specs=[smem] * 3 + [vmem] * len(arrays),
            out_specs=[vmem] * len(outs),
            scratch_shapes=scratch(*held),
            compiler_params=params,
            cost_estimate=pl.CostEstimate(
                flops=slots // 4 * 32 * size**3, bytes_accessed=8 * size * size * slots, transcendentals=0),
            name=name,
        )(slot_rows, slot_cols, live_count, *arrays)

    params = pltpu.CompilerParams(vmem_limit_bytes=24 * 1024 * 1024)
    edge = cols_here // LANES
    rim = size // LANES
    plane = f32(2, size, size)

    update, probe_sum, amps = call(
        inner_kernel, "inner_slots", [f32(2, edge, rows_here, LANES), plane, jax.ShapeDtypeStruct(amps.shape, amps.dtype)],
        (edge, rows_here, 1), object_field, probe, amps, mats)

    right_top = tie(right_top, probe_sum)
    corner = passed_along(right_top, "tile", -1)

    update, probe_sum, top_part, side_part, corner_part = call(
        right_kernel, "right_slots",
        [f32(2, edge, rows_here + size, LANES), plane, f32(2, rim, size, LANES),
         f32(2, rim, rows_here - size, LANES), f32(2, rim, size, LANES)],
        (edge + rim, rows_here + size, 2),
        object_field, lower, right_top, right_side, corner, probe, amps, mats, update, probe_sum)

    corner_back = passed_along(corner_part, "tile", 1)
    side_back = passed_along(side_part, "pos", 1)

    update, low_part, probe_sum = call(
        lower_kernel, "lower_slots",
        [f32(2, edge, rows_here + size, LANES), f32(2, edge, size, LANES), plane],
        (edge, rows_here + size, 1), object_field, lower, probe, amps, mats, update, probe_sum)

    low_back = passed_along(low_part, "tile", 1)
    top_back = passed_along(top_part + tie(corner_back, probe_sum), "pos", 1)

    tile_steps = masks_of("tile")
    pos_steps = masks_of("pos")[::-1]

    def sum_all(value):
        for step in tile_steps + pos_steps[:-2]:
            value = halve(value, *step)
        for step in pos_steps[-2:]:
            value = value + partner(value, *step)
        value = value * (1.0 / math.sqrt(lax.axis_size("pos") * lax.axis_size("tile") * slots))
        for step in pos_steps[:-2][::-1] + tile_steps[::-1]:
            value = rejoin(value, *step)
        return value

    probe_grad = lax.cond(live_count[0] >= 1, sum_all, jnp.zeros_like, probe_sum.reshape(2 * size, size))

    object_new = pl.pallas_call(
        finish_kernel,
        out_shape=f32(2, rows_here, cols_here),
        in_specs=[vmem] * 6,
        out_specs=vmem,
        compiler_params=params,
        name="finish",
    )(object_field, update, low_back, top_back, side_back, probe)
    return (object_new, probe_grad.reshape(2, size, size))


def solution(mesh):
    return jax.shard_map(
        shards,
        mesh=mesh,
        in_specs=(
            P(None, "tile", "pos"),
            P(),
            P("tile", "pos", None, None, None),
            P("tile", "pos", None),
            P("tile", "pos", None),
            P("tile", "pos"),
        ),
        out_specs=(P(None, "tile", "pos"), P()),
        check_vma=False,
    )
```

```python
import math

import jax
import jax.numpy as jnp
import numpy as np
from jax import lax
from jax.experimental import pallas as pl
from jax.experimental.pallas import tpu as pltpu
from jax.sharding import PartitionSpec as P

LANES = 128
STEP = 32
GROUP = 4


def passed_along(block, axis, distance):
    devices = range(lax.axis_size(axis))
    route = [(i - distance, i) for i in devices if i - distance in devices]
    return lax.ppermute(block, axis, route)


def dft_blocks(points):
    indices = np.arange(points)
    angles = (indices[:, None] * indices[None, :] % points) * (2.0 * math.pi / points)
    factor = 1.0 / math.sqrt(points)
    table_re, table_im = np.cos(angles) * factor, -np.sin(angles) * factor

    def left(rows, cols, sign):
        re, im = table_re[rows, cols], sign * table_im[rows, cols]
        return np.block([[re, -im], [im, re]])

    def right(rows, cols, sign):
        re, im = table_re[rows, cols], sign * table_im[rows, cols]
        return np.block([[re, im], [-im, re]])

    low, even, odd = slice(0, points // 2), slice(0, None, 2), slice(1, None, 2)
    order = np.concatenate([indices[even], indices[odd]])
    sort = np.zeros((points, points))
    sort[indices, order] = 1.0
    return np.stack([
        left(even, low, 1), left(odd, low, 1), right(low, even, 1), right(low, odd, 1),
        left(low, even, -1), left(low, odd, -1), right(even, low, -1), right(odd, low, -1),
        sort, sort.T,
    ]).astype(jnp.bfloat16)


def dot(a, b):
    return jnp.dot(a, b, preferred_element_type=jnp.float32)


def collect(keep, slot_total, order_ref):
    def look(slot, found):
        order_ref[found] = slot
        return found + keep(slot).astype(jnp.int32)

    found = lax.fori_loop(0, slot_total, look, jnp.int32(0))
    last = order_ref[jnp.maximum(found - 1, 0)]
    for extra in range(GROUP - 1):
        order_ref[found + extra] = last
    return found


def run_slots(found, order_ref, rows_ref, cols_ref, probe_ref, amp_ref, mats,
              field, update, probe_sum, scratch):
    size = probe_ref.shape[1]
    half = size // 2
    bf16 = jnp.bfloat16
    patch, xs, far, gs = scratch

    def place(slot):
        col = cols_ref[slot]
        return rows_ref[slot], col // LANES, col % LANES

    def times(re, im, other_re, other_im):
        return re * other_re - im * other_im, re * other_im + im * other_re

    def read(which, slot):
        row, base, shift = place(slot)
        own = lax.broadcasted_iota(jnp.int32, (STEP, LANES), 1) < LANES - shift
        for at in range(0, half, STEP):
            rounded = [[None, None], [None, None]]
            for low in range(2):
                top = low * half + at
                rows = slice(top, top + STEP)
                part = [[None, None], [None, None]]
                for plane in range(2):
                    rolled = [pltpu.roll(field[plane, base + k, pl.ds(row + top, STEP), :], LANES - shift, 1) for k in range(3)]
                    for block in range(2):
                        part[block][plane] = jnp.where(own, rolled[block], rolled[block + 1])
                        patch[which, plane, rows, block * LANES:(block + 1) * LANES] = part[block][plane]
                for block in range(2):
                    cols = slice(block * LANES, (block + 1) * LANES)
                    re, im = times(probe_ref[0, rows, cols], probe_ref[1, rows, cols], *part[block])
                    rounded[block][low] = (re.astype(bf16), im.astype(bf16))
            for block in range(2):
                cols = slice(which * size + block * LANES, which * size + (block + 1) * LANES)
                for plane in range(2):
                    up, low = rounded[block][0][plane], rounded[block][1][plane]
                    rows = slice(plane * half + at, plane * half + at + STEP)
                    xs[0, rows, cols] = up + low
                    xs[1, rows, cols] = up - low

    def run_group(count, first, all_live):
        wide = slice(0, count * size)
        slots = [order_ref[first + i] for i in range(count)]
        for which in range(count):
            read(which, slots[which])
        near = [dot(mats[parity], xs[parity, :, wide]).astype(bf16) for parity in range(2)]
        folds = [[], []]
        for which in range(count):
            for parity in range(2):
                left = near[parity][:, which * size:which * size + half]
                right = near[parity][:, which * size + half:(which + 1) * size]
                for sign, both in enumerate((left + right, left - right)):
                    folds[sign].append(jnp.concatenate([both[:half], both[half:]], axis=1))
        for sign in range(2):
            far[sign, wide, :] = dot(jnp.concatenate(folds[sign], axis=0), mats[2 + sign])
        for which in range(count):
            for at in range(0, size, STEP):
                rows = slice(which * size + at, which * size + at + STEP)
                for block in range(2):
                    re = far[block, rows, :half]
                    im = far[block, rows, half:]
                    amp = amp_ref[slots[which], at:at + STEP, block * LANES:(block + 1) * LANES].astype(jnp.float32)
                    ratio = amp * lax.rsqrt(re * re + im * im + 0.25)
                    down = at % half
                    cols = slice(which * size + block * LANES, which * size + (block + 1) * LANES)
                    gs[at // half, down:down + STEP, cols] = (re * ratio).astype(bf16)
                    gs[at // half, half + down:half + down + STEP, cols] = (im * ratio).astype(bf16)
        even = dot(mats[4], gs[0, :, wide])
        odd = dot(mats[5], gs[1, :, wide])
        back = (even + odd).astype(bf16), (even - odd).astype(bf16)
        sums = []
        for parity in range(2):
            parts = []
            for which in range(count):
                cols = slice(which * size + parity * half, which * size + (parity + 1) * half)
                for value in back:
                    parts.append(jnp.concatenate([value[:half, cols], value[half:, cols]], axis=1))
            sums.append(dot(jnp.concatenate(parts, axis=0), mats[6 + parity]))
        places = [place(slot) for slot in slots]
        weights = [None] * count if all_live else [None] + [jnp.where(first + i < found, 1.0, 0.0).astype(jnp.float32) for i in range(1, count)]
        for at in range(0, size, STEP):
            rows = slice(at, at + STEP)
            terms = [[[], []] for _ in range(count)]
            for block in range(2):
                cols = slice(block * LANES, (block + 1) * LANES)
                probe_re = probe_ref[0, rows, cols]
                probe_im = probe_ref[1, rows, cols]
                total = None
                for which in range(count):
                    patch_re = patch[which, 0, rows, cols]
                    patch_im = patch[which, 1, rows, cols]
                    delta = []
                    for plane, value in enumerate(times(probe_re, probe_im, patch_re, patch_im)):
                        a = sums[0][which * size + at:which * size + at + STEP, plane * half:(plane + 1) * half]
                        b = sums[1][which * size + at:which * size + at + STEP, plane * half:(plane + 1) * half]
                        value = (a + b if block == 0 else a - b) - value
                        delta.append(value if weights[which] is None else value * weights[which])
                    shift = places[which][2]
                    terms[which][0].append(pltpu.roll(probe_re * delta[0] + probe_im * delta[1], shift, 1))
                    terms[which][1].append(pltpu.roll(probe_re * delta[1] - probe_im * delta[0], shift, 1))
                    own_sum = patch_re * delta[0] + patch_im * delta[1], patch_re * delta[1] - patch_im * delta[0]
                    total = own_sum if total is None else (total[0] + own_sum[0], total[1] + own_sum[1])
                probe_sum[0, rows, cols] += total[0]
                probe_sum[1, rows, cols] += total[1]
            for which in range(count):
                row, base, shift = places[which]
                own = lax.broadcasted_iota(jnp.int32, (STEP, LANES), 1) >= shift
                for plane in range(2):
                    first, second = terms[which][plane]
                    update[plane, base, pl.ds(row + at, STEP), :] += jnp.where(own, first, 0.0)
                    update[plane, base + 1, pl.ds(row + at, STEP), :] += jnp.where(own, second, first)
                    update[plane, base + 2, pl.ds(row + at, STEP), :] += jnp.where(own, 0.0, second)

    def whole_group(step, carry):
        run_group(GROUP, step * GROUP, True)
        return carry

    def pair(step, carry):
        run_group(2, found // GROUP * GROUP + step * 2, False)
        return carry

    lax.fori_loop(0, found // GROUP, whole_group, 0)
    lax.fori_loop(0, (found % GROUP + 1) // 2, pair, 0)


def put(into, row, col, value):
    rows, cols = value.shape[1:]
    for block in range(cols // LANES):
        into[:, col // LANES + block, row:row + rows, :] = value[:, :, block * LANES:(block + 1) * LANES]


def inner_kernel(rows_ref, cols_ref, count_ref, block_ref, probe_ref, amps_ref, mats,
                 update, probe_sum, amp_ref, scale_ref, order_ref, field, *scratch):
    size = probe_ref.shape[1]
    rows_here, cols_here = block_ref.shape[1:]
    put(field, 0, 0, block_ref)
    update[...] = jnp.zeros_like(update)
    probe_sum[...] = jnp.zeros_like(probe_sum)
    probe_re = probe_ref[0]
    probe_im = probe_ref[1]
    power = jnp.mean(probe_re * probe_re + probe_im * probe_im) + 1e-06
    scale_ref[...] = jnp.ones_like(scale_ref) / power
    live = count_ref[0, 0]
    total = rows_ref.shape[0]
    batch = math.gcd(4, total)

    def sort_amps(step, carry):
        taken = [amps_ref[step * batch + i] for i in range(batch)]
        taken = [dot(mats[8], value).astype(jnp.bfloat16) for value in taken]
        for i in range(batch):
            amp_ref[step * batch + i] = dot(taken[i], mats[9]).astype(jnp.bfloat16)
        return carry

    lax.fori_loop(0, (live + batch - 1) // batch, sort_amps, 0)

    def keep(slot):
        return (slot < live) & (cols_ref[slot] < cols_here - size) & (rows_ref[slot] <= rows_here - size)

    found = collect(keep, total, order_ref)
    run_slots(found, order_ref, rows_ref, cols_ref, probe_ref, amp_ref, mats, field, update, probe_sum, scratch)


def lower_kernel(rows_ref, cols_ref, count_ref, block_ref, lower_ref, probe_ref, amp_ref, mats, update_in, probe_in,
                 update, probe_sum, order_ref, field, *scratch):
    size = probe_ref.shape[1]
    rows_here, cols_here = block_ref.shape[1:]
    put(field, 0, 0, block_ref)
    put(field, rows_here, 0, lower_ref)
    update[:, :, :rows_here, :] = update_in[...]
    update[:, :, rows_here:, :] = jnp.zeros((2, cols_here // LANES, size, LANES), jnp.float32)
    probe_sum[...] = probe_in[...]
    live = count_ref[0, 0]

    def keep(slot):
        return (slot < live) & (cols_ref[slot] < cols_here - size) & (rows_ref[slot] > rows_here - size)

    found = collect(keep, rows_ref.shape[0], order_ref)
    run_slots(found, order_ref, rows_ref, cols_ref, probe_ref, amp_ref, mats, field, update, probe_sum, scratch)


def right_kernel(rows_ref, cols_ref, count_ref, block_ref, lower_ref, top_ref, side_ref, corner_ref,
                 probe_ref, amp_ref, mats, update_in, probe_in,
                 own_out, low_out, top_out, side_out, corner_out, kept_out, given_out, alive_ref, order_ref, field, update, probe_sum, *scratch):
    size = probe_ref.shape[1]
    rows_here, cols_here = block_ref.shape[1:]
    edge = cols_here // LANES
    put(field, 0, 0, block_ref)
    put(field, rows_here, 0, lower_ref)
    put(field, 0, cols_here, top_ref)
    put(field, size, cols_here, side_ref)
    put(field, rows_here, cols_here, corner_ref)
    update[:, :edge, :, :] = update_in[...]
    update[:, edge:, :, :] = jnp.zeros((2, size // LANES, rows_here + size, LANES), jnp.float32)
    probe_sum[...] = probe_in[...]
    live = count_ref[0, 0]
    found = collect(lambda slot: (slot < live) & (cols_ref[slot] >= cols_here - size), rows_ref.shape[0], order_ref)
    run_slots(found, order_ref, rows_ref, cols_ref, probe_ref, amp_ref, mats, field, update, probe_sum, scratch)
    corner_out[...] = update[:, edge:, rows_here:, :]
    side_out[...] = update[:, edge:, size:rows_here, :]
    top_out[...] = update[:, edge:, :size, :]
    low_out[...] = update[:, :edge, rows_here:, :]
    own_out[...] = update[:, :edge, :rows_here, :]
    half = lax.rem(lax.axis_index("tile"), 2)
    alive_ref[0] = live
    kept_out[...] = probe_sum[half]
    given_out[...] = probe_sum[1 - half]


def cut_kernel(block, top_out, side_out, low_out, sems):
    size = top_out.shape[1]
    copies = [
        pltpu.make_async_copy(block.at[:, :size, :size], top_out, sems.at[0]),
        pltpu.make_async_copy(block.at[:, size:, :size], side_out, sems.at[1]),
        pltpu.make_async_copy(block.at[:, :size, :], low_out, sems.at[2]),
    ]
    for copy in copies:
        copy.start()
    for copy in copies:
        copy.wait()


def tie_kernel(value_in, other_in, value_out):
    pass


def tie(value, other):
    anywhere = pl.BlockSpec(memory_space=pl.ANY)
    return pl.pallas_call(
        tie_kernel,
        out_shape=jax.ShapeDtypeStruct(value.shape, value.dtype),
        in_specs=[anywhere] * 2,
        out_specs=anywhere,
        input_output_aliases={0: 0},
        compiler_params=pltpu.CompilerParams(vmem_limit_bytes=1024 * 1024),
        name="tie",
    )(value, other)


def finish_kernel(block_ref, update, low_ref, top_ref, side_ref, scale_ref, out_ref):
    size = low_ref.shape[2]
    scale = scale_ref[0:1, :]
    for plane in range(2):
        for block in range(update.shape[1]):
            cols = slice(block * LANES, (block + 1) * LANES)
            top = update[plane, block, :size, :] + low_ref[plane, block]
            side = update[plane, block, size:, :]
            if block < top_ref.shape[1]:
                top = top + top_ref[plane, block]
                side = side + side_ref[plane, block]
            out_ref[plane, :size, cols] = block_ref[plane, :size, cols] + top * scale
            out_ref[plane, size:, cols] = block_ref[plane, size:, cols] + side * scale


def partner(block, axis, mask):
    return lax.ppermute(block, axis, [(i, i ^ mask) for i in range(lax.axis_size(axis))])


def is_low(axis, mask):
    return lax.axis_index(axis) // mask % 2 == 0


def halve(value, axis, mask):
    half = value.shape[0] // 2
    low = is_low(axis, mask)
    kept = jnp.where(low, value[:half], value[half:])
    given = jnp.where(low, value[half:], value[:half])
    return kept + partner(given, axis, mask)


def rejoin(value, axis, mask):
    other = partner(value, axis, mask)
    return jnp.where(is_low(axis, mask), jnp.concatenate([value, other]), jnp.concatenate([other, value]))


def masks_of(axis):
    masks = []
    while 2 ** len(masks) < lax.axis_size(axis):
        masks.append((axis, 2 ** len(masks)))
    return masks


def shards(object_field, probe, amplitudes, corner_rows, corner_cols, counts):
    size = probe.shape[1]
    rows_here = object_field.shape[1]
    cols_here = object_field.shape[2]
    slots = corner_rows.shape[2]
    mats = jnp.asarray(dft_blocks(size))
    slot_rows = corner_rows.reshape(slots)
    slot_cols = corner_cols.reshape(slots)
    live_count = counts
    amps = amplitudes.reshape(slots, size, size)

    smem = pl.BlockSpec(memory_space=pltpu.SMEM)
    vmem = pl.BlockSpec(memory_space=pltpu.VMEM)

    def f32(*shape):
        return jax.ShapeDtypeStruct(shape, jnp.float32)

    def scratch(blocks, rows, kept):
        held = pltpu.VMEM((2, blocks, rows, LANES), jnp.float32)
        return [pltpu.SMEM((slots + GROUP,), jnp.int32)] + [held] * kept + [
            pltpu.VMEM((GROUP, 2, size, size), jnp.float32),
            pltpu.VMEM((2, size, GROUP * size), jnp.bfloat16),
            pltpu.VMEM((2, GROUP * size, size), jnp.float32),
            pltpu.VMEM((2, size, GROUP * size), jnp.bfloat16),
        ]

    def call(kernel, name, mib, outs, held, *arrays, flags=0):
        return pl.pallas_call(
            kernel,
            out_shape=outs,
            in_specs=[smem] * 3 + [vmem] * len(arrays),
            out_specs=[vmem] * (len(outs) - flags) + [smem] * flags,
            scratch_shapes=[*scratch(*held[:3])[:1 + held[2]], *held[3:], *scratch(*held[:3])[1 + held[2]:]],
            compiler_params=pltpu.CompilerParams(vmem_limit_bytes=mib * 1024 * 1024),
            cost_estimate=pl.CostEstimate(
                flops=slots // 4 * 32 * size**3, bytes_accessed=8 * size * size * slots, transcendentals=0),
            name=name,
        )(slot_rows, slot_cols, live_count, *arrays)

    edge = cols_here // LANES
    rim = size // LANES
    plane = f32(2, size, size)
    anywhere = pl.BlockSpec(memory_space=pl.ANY)
    top_cut, side_cut, low_cut = pl.pallas_call(
        cut_kernel,
        out_shape=(plane, f32(2, rows_here - size, size), f32(2, size, cols_here)),
        in_specs=[anywhere],
        out_specs=(anywhere,) * 3,
        scratch_shapes=[pltpu.SemaphoreType.DMA((3,))],
        compiler_params=pltpu.CompilerParams(vmem_limit_bytes=1024 * 1024),
        name="cut",
    )(object_field)
    right_top = passed_along(top_cut, "pos", -1)
    right_side = passed_along(side_cut, "pos", -1)
    lower = passed_along(low_cut, "tile", -1)

    tile_steps = masks_of("tile")
    pos_steps = masks_of("pos")[::-1]
    update, probe_sum, amps, scale = call(
        inner_kernel, "inner_slots", 20,
        [f32(2, edge, rows_here, LANES), plane, jax.ShapeDtypeStruct(amps.shape, amps.dtype), f32(8, LANES)],
        (edge, rows_here, 1), object_field, probe, amps, mats)

    right_top = tie(right_top, probe_sum)
    corner = passed_along(right_top, "tile", -1)

    update, probe_sum = call(
        lower_kernel, "lower_slots", 20, [f32(2, edge, rows_here + size, LANES), plane],
        (edge, rows_here + size, 1), object_field, lower, probe, amps, mats, update, probe_sum)

    own_part, low_part, top_part, side_part, corner_part, kept, given, alive = call(
        right_kernel, "right_slots", 26,
        [f32(2, edge, rows_here, LANES), f32(2, edge, size, LANES), f32(2, rim, size, LANES),
         f32(2, rim, rows_here - size, LANES), f32(2, rim, size, LANES), f32(size, size), f32(size, size),
         jax.ShapeDtypeStruct((1,), jnp.int32)],
        (edge + rim, rows_here + size, 2, pltpu.VMEM((2, size, size), jnp.float32)),
        object_field, lower, right_top, right_side, corner, probe, amps, mats, update, probe_sum, flags=1)

    def sum_first(kept, given):
        value = kept + partner(given, *tile_steps[0])
        for step in tile_steps[1:]:
            value = halve(value, *step)
        return value

    def sum_rest(value):
        for step in pos_steps[:-2]:
            value = halve(value, *step)
        for step in pos_steps[-2:]:
            value = value + partner(value, *step)
        value = value * (1.0 / math.sqrt(lax.axis_size("pos") * lax.axis_size("tile") * slots))
        for step in pos_steps[:-2][::-1] + tile_steps[::-1]:
            value = rejoin(value, *step)
        return value

    corner_back = passed_along(corner_part, "tile", 1)
    side_back = passed_along(side_part, "pos", 1)
    low_back = passed_along(low_part, "tile", 1)
    share = 2 * size // lax.axis_size("tile")
    summed = lax.cond(alive[0] >= 1, sum_first, lambda kept, given: kept[:share], kept, given)
    top_back = passed_along(top_part + tie(corner_back, summed), "pos", 1)
    probe_grad = lax.cond(alive[0] >= 1, sum_rest, lambda v: jnp.zeros((2 * size, size), jnp.float32), summed)

    object_new = pl.pallas_call(
        finish_kernel,
        out_shape=f32(2, rows_here, cols_here),
        in_specs=[vmem] * 6,
        out_specs=vmem,
        compiler_params=pltpu.CompilerParams(vmem_limit_bytes=8 * 1024 * 1024),
        name="finish",
    )(object_field, own_part, low_back, top_back, side_back, scale)
    return (object_new, probe_grad.reshape(2, size, size))


def solution(mesh):
    return jax.shard_map(
        shards,
        mesh=mesh,
        in_specs=(
            P(None, "tile", "pos"),
            P(),
            P("tile", "pos", None, None, None),
            P("tile", "pos", None),
            P("tile", "pos", None),
            P("tile", "pos"),
        ),
        out_specs=(P(None, "tile", "pos"), P()),
        check_vma=False,
    )
```

```python
import math

import jax
import jax.numpy as jnp
import numpy as np
from jax import lax
from jax.experimental import pallas as pl
from jax.experimental.pallas import tpu as pltpu
from jax.sharding import PartitionSpec as P

LANES = 128
STEP = 32
GROUP = 4


def passed_along(block, axis, distance):
    devices = range(lax.axis_size(axis))
    route = [(i - distance, i) for i in devices if i - distance in devices]
    return lax.ppermute(block, axis, route)


def dft_blocks(points):
    indices = np.arange(points)
    angles = (indices[:, None] * indices[None, :] % points) * (2.0 * math.pi / points)
    factor = 1.0 / math.sqrt(points)
    table_re, table_im = np.cos(angles) * factor, -np.sin(angles) * factor

    def left(rows, cols, sign):
        re, im = table_re[rows, cols], sign * table_im[rows, cols]
        return np.block([[re, -im], [im, re]])

    def right(rows, cols, sign):
        re, im = table_re[rows, cols], sign * table_im[rows, cols]
        return np.block([[re, im], [-im, re]])

    low, even, odd = slice(0, points // 2), slice(0, None, 2), slice(1, None, 2)
    order = np.concatenate([indices[even], indices[odd]])
    sort = np.zeros((points, points))
    sort[indices, order] = 1.0
    return np.stack([
        left(even, low, 1), left(odd, low, 1), right(low, even, 1), right(low, odd, 1),
        left(low, even, -1), left(low, odd, -1), right(even, low, -1), right(odd, low, -1),
        sort, sort.T,
    ]).astype(jnp.bfloat16)


def dot(a, b):
    return jnp.dot(a, b, preferred_element_type=jnp.float32)


def collect(keep, slot_total, order_ref):
    def look(slot, found):
        order_ref[found] = slot
        return found + keep(slot).astype(jnp.int32)

    found = lax.fori_loop(0, slot_total, look, jnp.int32(0))
    last = order_ref[jnp.maximum(found - 1, 0)]
    for extra in range(GROUP - 1):
        order_ref[found + extra] = last
    return found


def run_slots(found, order_ref, rows_ref, cols_ref, probe_ref, amp_ref, mats,
              field, update, probe_sum, scratch):
    size = probe_ref.shape[1]
    half = size // 2
    bf16 = jnp.bfloat16
    patch, xs, far, gs = scratch

    def place(slot):
        col = cols_ref[slot]
        return rows_ref[slot], col // LANES, col % LANES

    def times(re, im, other_re, other_im):
        return re * other_re - im * other_im, re * other_im + im * other_re

    def read(which, slot):
        row, base, shift = place(slot)
        own = lax.broadcasted_iota(jnp.int32, (STEP, LANES), 1) < LANES - shift
        for at in range(0, half, STEP):
            rounded = [[None, None], [None, None]]
            for low in range(2):
                top = low * half + at
                rows = slice(top, top + STEP)
                part = [[None, None], [None, None]]
                for plane in range(2):
                    rolled = [pltpu.roll(field[plane, base + k, pl.ds(row + top, STEP), :], LANES - shift, 1) for k in range(3)]
                    for block in range(2):
                        part[block][plane] = jnp.where(own, rolled[block], rolled[block + 1])
                        patch[which, plane, rows, block * LANES:(block + 1) * LANES] = part[block][plane]
                for block in range(2):
                    cols = slice(block * LANES, (block + 1) * LANES)
                    re, im = times(probe_ref[0, rows, cols], probe_ref[1, rows, cols], *part[block])
                    rounded[block][low] = (re.astype(bf16), im.astype(bf16))
            for block in range(2):
                cols = slice(which * size + block * LANES, which * size + (block + 1) * LANES)
                for plane in range(2):
                    up, low = rounded[block][0][plane], rounded[block][1][plane]
                    rows = slice(plane * half + at, plane * half + at + STEP)
                    xs[0, rows, cols] = up + low
                    xs[1, rows, cols] = up - low

    def run_group(count, first, all_live):
        wide = slice(0, count * size)
        slots = [order_ref[first + i] for i in range(count)]
        for which in range(count):
            read(which, slots[which])
        near = [dot(mats[parity], xs[parity, :, wide]).astype(bf16) for parity in range(2)]
        folds = [[], []]
        for which in range(count):
            for parity in range(2):
                left = near[parity][:, which * size:which * size + half]
                right = near[parity][:, which * size + half:(which + 1) * size]
                for sign, both in enumerate((left + right, left - right)):
                    folds[sign].append(jnp.concatenate([both[:half], both[half:]], axis=1))
        for sign in range(2):
            far[sign, wide, :] = dot(jnp.concatenate(folds[sign], axis=0), mats[2 + sign])
        for which in range(count):
            for at in range(0, size, STEP):
                rows = slice(which * size + at, which * size + at + STEP)
                for block in range(2):
                    re = far[block, rows, :half]
                    im = far[block, rows, half:]
                    amp = amp_ref[slots[which], at:at + STEP, block * LANES:(block + 1) * LANES].astype(jnp.float32)
                    ratio = amp * lax.rsqrt(re * re + im * im + 0.25)
                    down = at % half
                    cols = slice(which * size + block * LANES, which * size + (block + 1) * LANES)
                    gs[at // half, down:down + STEP, cols] = (re * ratio).astype(bf16)
                    gs[at // half, half + down:half + down + STEP, cols] = (im * ratio).astype(bf16)
        even = dot(mats[4], gs[0, :, wide])
        odd = dot(mats[5], gs[1, :, wide])
        back = (even + odd).astype(bf16), (even - odd).astype(bf16)
        sums = []
        for parity in range(2):
            parts = []
            for which in range(count):
                cols = slice(which * size + parity * half, which * size + (parity + 1) * half)
                for value in back:
                    parts.append(jnp.concatenate([value[:half, cols], value[half:, cols]], axis=1))
            sums.append(dot(jnp.concatenate(parts, axis=0), mats[6 + parity]))
        places = [place(slot) for slot in slots]
        weights = [None] * count if all_live else [None] + [jnp.where(first + i < found, 1.0, 0.0).astype(jnp.float32) for i in range(1, count)]
        for at in range(0, size, STEP):
            rows = slice(at, at + STEP)
            terms = [[[], []] for _ in range(count)]
            for block in range(2):
                cols = slice(block * LANES, (block + 1) * LANES)
                probe_re = probe_ref[0, rows, cols]
                probe_im = probe_ref[1, rows, cols]
                total = None
                for which in range(count):
                    patch_re = patch[which, 0, rows, cols]
                    patch_im = patch[which, 1, rows, cols]
                    delta = []
                    for plane, value in enumerate(times(probe_re, probe_im, patch_re, patch_im)):
                        a = sums[0][which * size + at:which * size + at + STEP, plane * half:(plane + 1) * half]
                        b = sums[1][which * size + at:which * size + at + STEP, plane * half:(plane + 1) * half]
                        value = (a + b if block == 0 else a - b) - value
                        delta.append(value if weights[which] is None else value * weights[which])
                    shift = places[which][2]
                    terms[which][0].append(pltpu.roll(probe_re * delta[0] + probe_im * delta[1], shift, 1))
                    terms[which][1].append(pltpu.roll(probe_re * delta[1] - probe_im * delta[0], shift, 1))
                    own_sum = patch_re * delta[0] + patch_im * delta[1], patch_re * delta[1] - patch_im * delta[0]
                    total = own_sum if total is None else (total[0] + own_sum[0], total[1] + own_sum[1])
                probe_sum[0, rows, cols] += total[0]
                probe_sum[1, rows, cols] += total[1]
            for which in range(count):
                row, base, shift = places[which]
                own = lax.broadcasted_iota(jnp.int32, (STEP, LANES), 1) >= shift
                for plane in range(2):
                    first, second = terms[which][plane]
                    update[plane, base, pl.ds(row + at, STEP), :] += jnp.where(own, first, 0.0)
                    update[plane, base + 1, pl.ds(row + at, STEP), :] += jnp.where(own, second, first)
                    update[plane, base + 2, pl.ds(row + at, STEP), :] += jnp.where(own, 0.0, second)

    def whole_group(step, carry):
        run_group(GROUP, step * GROUP, True)
        return carry

    def pair(step, carry):
        run_group(2, found // GROUP * GROUP + step * 2, False)
        return carry

    lax.fori_loop(0, found // GROUP, whole_group, 0)
    lax.fori_loop(0, (found % GROUP + 1) // 2, pair, 0)


def put(into, row, col, value):
    rows, cols = value.shape[1:]
    for block in range(cols // LANES):
        into[:, col // LANES + block, row:row + rows, :] = value[:, :, block * LANES:(block + 1) * LANES]


def inner_kernel(rows_ref, cols_ref, count_ref, block_ref, probe_ref, amps_ref, mats,
                 update, probe_sum, amp_ref, scale_ref, order_ref, field, *scratch):
    size = probe_ref.shape[1]
    rows_here, cols_here = block_ref.shape[1:]
    put(field, 0, 0, block_ref)
    update[...] = jnp.zeros_like(update)
    probe_sum[...] = jnp.zeros_like(probe_sum)
    probe_re = probe_ref[0]
    probe_im = probe_ref[1]
    power = jnp.mean(probe_re * probe_re + probe_im * probe_im) + 1e-06
    scale_ref[...] = jnp.ones_like(scale_ref) / power
    live = count_ref[0, 0]
    total = rows_ref.shape[0]
    batch = math.gcd(4, total)

    def sort_amps(step, carry):
        taken = [amps_ref[step * batch + i] for i in range(batch)]
        taken = [dot(mats[8], value).astype(jnp.bfloat16) for value in taken]
        for i in range(batch):
            amp_ref[step * batch + i] = dot(taken[i], mats[9]).astype(jnp.bfloat16)
        return carry

    lax.fori_loop(0, (live + batch - 1) // batch, sort_amps, 0)

    def keep(slot):
        return (slot < live) & (cols_ref[slot] < cols_here - size) & (rows_ref[slot] <= rows_here - size)

    found = collect(keep, total, order_ref)
    run_slots(found, order_ref, rows_ref, cols_ref, probe_ref, amp_ref, mats, field, update, probe_sum, scratch)


def lower_kernel(rows_ref, cols_ref, count_ref, block_ref, lower_ref, probe_ref, amp_ref, mats, update_in, probe_in,
                 update, probe_sum, order_ref, field, *scratch):
    size = probe_ref.shape[1]
    rows_here, cols_here = block_ref.shape[1:]
    put(field, 0, 0, block_ref)
    put(field, rows_here, 0, lower_ref)
    update[:, :, :rows_here, :] = update_in[...]
    update[:, :, rows_here:, :] = jnp.zeros((2, cols_here // LANES, size, LANES), jnp.float32)
    probe_sum[...] = probe_in[...]
    live = count_ref[0, 0]

    def keep(slot):
        return (slot < live) & (cols_ref[slot] < cols_here - size) & (rows_ref[slot] > rows_here - size)

    found = collect(keep, rows_ref.shape[0], order_ref)
    run_slots(found, order_ref, rows_ref, cols_ref, probe_ref, amp_ref, mats, field, update, probe_sum, scratch)


def right_kernel(rows_ref, cols_ref, count_ref, block_ref, lower_ref, top_ref, side_ref, corner_ref,
                 probe_ref, amp_ref, mats, update_in, probe_in,
                 own_out, low_out, top_out, side_out, corner_out, kept_out, given_out, alive_ref, order_ref, field, update, probe_sum, *scratch):
    size = probe_ref.shape[1]
    rows_here, cols_here = block_ref.shape[1:]
    edge = cols_here // LANES
    put(field, 0, 0, block_ref)
    put(field, rows_here, 0, lower_ref)
    put(field, 0, cols_here, top_ref)
    put(field, size, cols_here, side_ref)
    put(field, rows_here, cols_here, corner_ref)
    update[:, :edge, :, :] = update_in[...]
    update[:, edge:, :, :] = jnp.zeros((2, size // LANES, rows_here + size, LANES), jnp.float32)
    probe_sum[...] = probe_in[...]
    live = count_ref[0, 0]
    found = collect(lambda slot: (slot < live) & (cols_ref[slot] >= cols_here - size), rows_ref.shape[0], order_ref)
    run_slots(found, order_ref, rows_ref, cols_ref, probe_ref, amp_ref, mats, field, update, probe_sum, scratch)
    corner_out[...] = update[:, edge:, rows_here:, :]
    side_out[...] = update[:, edge:, size:rows_here, :]
    top_out[...] = update[:, edge:, :size, :]
    low_out[...] = update[:, :edge, rows_here:, :]
    own_out[...] = update[:, :edge, :rows_here, :]
    half = lax.rem(lax.axis_index("tile"), 2)
    alive_ref[0] = live
    kept_out[...] = probe_sum[half]
    given_out[...] = probe_sum[1 - half]


def cut_kernel(block, top_out, side_out, low_out, sems):
    size = top_out.shape[1]
    copies = [
        pltpu.make_async_copy(block.at[:, :size, :size], top_out, sems.at[0]),
        pltpu.make_async_copy(block.at[:, size:, :size], side_out, sems.at[1]),
        pltpu.make_async_copy(block.at[:, :size, :], low_out, sems.at[2]),
    ]
    for copy in copies:
        copy.start()
    for copy in copies:
        copy.wait()


def tie_kernel(value_in, other_in, value_out):
    pass


def tie(value, other):
    anywhere = pl.BlockSpec(memory_space=pl.ANY)
    return pl.pallas_call(
        tie_kernel,
        out_shape=jax.ShapeDtypeStruct(value.shape, value.dtype),
        in_specs=[anywhere] * 2,
        out_specs=anywhere,
        input_output_aliases={0: 0},
        compiler_params=pltpu.CompilerParams(vmem_limit_bytes=1024 * 1024),
        name="tie",
    )(value, other)


def finish_kernel(block_ref, update, low_ref, top_ref, side_ref, scale_ref, out_ref):
    size = low_ref.shape[2]
    scale = scale_ref[0:1, :]
    for plane in range(2):
        for block in range(update.shape[1]):
            cols = slice(block * LANES, (block + 1) * LANES)
            top = update[plane, block, :size, :] + low_ref[plane, block]
            side = update[plane, block, size:, :]
            if block < top_ref.shape[1]:
                top = top + top_ref[plane, block]
                side = side + side_ref[plane, block]
            out_ref[plane, :size, cols] = block_ref[plane, :size, cols] + top * scale
            out_ref[plane, size:, cols] = block_ref[plane, size:, cols] + side * scale


def partner(block, axis, mask):
    return lax.ppermute(block, axis, [(i, i ^ mask) for i in range(lax.axis_size(axis))])


def is_low(axis, mask):
    return lax.axis_index(axis) // mask % 2 == 0


def halve(value, axis, mask):
    half = value.shape[0] // 2
    low = is_low(axis, mask)
    kept = jnp.where(low, value[:half], value[half:])
    given = jnp.where(low, value[half:], value[:half])
    return kept + partner(given, axis, mask)


def rejoin(value, axis, mask):
    other = partner(value, axis, mask)
    return jnp.where(is_low(axis, mask), jnp.concatenate([value, other]), jnp.concatenate([other, value]))


def masks_of(axis):
    masks = []
    while 2 ** len(masks) < lax.axis_size(axis):
        masks.append((axis, 2 ** len(masks)))
    return masks


def shards(object_field, probe, amplitudes, corner_rows, corner_cols, counts):
    size = probe.shape[1]
    rows_here = object_field.shape[1]
    cols_here = object_field.shape[2]
    slots = corner_rows.shape[2]
    mats = jnp.asarray(dft_blocks(size))
    slot_rows = corner_rows.reshape(slots)
    slot_cols = corner_cols.reshape(slots)
    live_count = counts
    amps = amplitudes.reshape(slots, size, size)

    smem = pl.BlockSpec(memory_space=pltpu.SMEM)
    vmem = pl.BlockSpec(memory_space=pltpu.VMEM)

    def f32(*shape):
        return jax.ShapeDtypeStruct(shape, jnp.float32)

    def scratch(blocks, rows, kept):
        held = pltpu.VMEM((2, blocks, rows, LANES), jnp.float32)
        return [pltpu.SMEM((slots + GROUP,), jnp.int32)] + [held] * kept + [
            pltpu.VMEM((GROUP, 2, size, size), jnp.float32),
            pltpu.VMEM((2, size, GROUP * size), jnp.bfloat16),
            pltpu.VMEM((2, GROUP * size, size), jnp.float32),
            pltpu.VMEM((2, size, GROUP * size), jnp.bfloat16),
        ]

    def call(kernel, name, mib, outs, held, *arrays, flags=0):
        return pl.pallas_call(
            kernel,
            out_shape=outs,
            in_specs=[smem] * 3 + [vmem] * len(arrays),
            out_specs=[vmem] * (len(outs) - flags) + [smem] * flags,
            scratch_shapes=[*scratch(*held[:3])[:1 + held[2]], *held[3:], *scratch(*held[:3])[1 + held[2]:]],
            compiler_params=pltpu.CompilerParams(vmem_limit_bytes=mib * 1024 * 1024),
            cost_estimate=pl.CostEstimate(
                flops=slots // 4 * 32 * size**3, bytes_accessed=8 * size * size * slots, transcendentals=0),
            name=name,
        )(slot_rows, slot_cols, live_count, *arrays)

    edge = cols_here // LANES
    rim = size // LANES
    plane = f32(2, size, size)
    anywhere = pl.BlockSpec(memory_space=pl.ANY)
    top_cut, side_cut, low_cut = pl.pallas_call(
        cut_kernel,
        out_shape=(plane, f32(2, rows_here - size, size), f32(2, size, cols_here)),
        in_specs=[anywhere],
        out_specs=(anywhere,) * 3,
        scratch_shapes=[pltpu.SemaphoreType.DMA((3,))],
        compiler_params=pltpu.CompilerParams(vmem_limit_bytes=1024 * 1024),
        name="cut",
    )(object_field)
    right_top = passed_along(top_cut, "pos", -1)
    right_side = passed_along(side_cut, "pos", -1)
    lower = passed_along(low_cut, "tile", -1)

    tile_steps = masks_of("tile")
    pos_steps = masks_of("pos")[::-1]
    update, probe_sum, amps, scale = call(
        inner_kernel, "inner_slots", 20,
        [f32(2, edge, rows_here, LANES), plane, jax.ShapeDtypeStruct(amps.shape, amps.dtype), f32(8, LANES)],
        (edge, rows_here, 1), object_field, probe, amps, mats)

    right_top = tie(right_top, probe_sum)
    corner = passed_along(right_top, "tile", -1)

    update, probe_sum = call(
        lower_kernel, "lower_slots", 20, [f32(2, edge, rows_here + size, LANES), plane],
        (edge, rows_here + size, 1), object_field, lower, probe, amps, mats, update, probe_sum)

    own_part, low_part, top_part, side_part, corner_part, kept, given, alive = call(
        right_kernel, "right_slots", 26,
        [f32(2, edge, rows_here, LANES), f32(2, edge, size, LANES), f32(2, rim, size, LANES),
         f32(2, rim, rows_here - size, LANES), f32(2, rim, size, LANES), f32(size, size), f32(size, size),
         jax.ShapeDtypeStruct((1,), jnp.int32)],
        (edge + rim, rows_here + size, 2, pltpu.VMEM((2, size, size), jnp.float32)),
        object_field, lower, right_top, right_side, corner, probe, amps, mats, update, probe_sum, flags=1)

    def sum_first(kept, given):
        value = kept + partner(given, *tile_steps[0])
        for step in tile_steps[1:]:
            value = halve(value, *step)
        return value

    def sum_rest(value):
        for step in pos_steps[:-3]:
            value = halve(value, *step)
        for step in pos_steps[-3:]:
            value = value + partner(value, *step)
        value = value * (1.0 / math.sqrt(lax.axis_size("pos") * lax.axis_size("tile") * slots))
        for step in pos_steps[:-3][::-1] + tile_steps[::-1]:
            value = rejoin(value, *step)
        return value

    corner_back = passed_along(corner_part, "tile", 1)
    side_back = passed_along(side_part, "pos", 1)
    low_back = passed_along(low_part, "tile", 1)
    share = 2 * size // lax.axis_size("tile")
    summed = lax.cond(alive[0] >= 1, sum_first, lambda kept, given: kept[:share], kept, given)
    top_back = passed_along(top_part + tie(corner_back, summed), "pos", 1)
    probe_grad = lax.cond(alive[0] >= 1, sum_rest, lambda v: jnp.zeros((2 * size, size), jnp.float32), summed)

    object_new = pl.pallas_call(
        finish_kernel,
        out_shape=f32(2, rows_here, cols_here),
        in_specs=[vmem] * 6,
        out_specs=vmem,
        compiler_params=pltpu.CompilerParams(vmem_limit_bytes=8 * 1024 * 1024),
        name="finish",
    )(object_field, own_part, low_back, top_back, side_back, scale)
    return (object_new, probe_grad.reshape(2, size, size))


def solution(mesh):
    return jax.shard_map(
        shards,
        mesh=mesh,
        in_specs=(
            P(None, "tile", "pos"),
            P(),
            P("tile", "pos", None, None, None),
            P("tile", "pos", None),
            P("tile", "pos", None),
            P("tile", "pos"),
        ),
        out_specs=(P(None, "tile", "pos"), P()),
        check_vma=False,
    )
```
